32 devices in a mesh: gx: 4 (over z), gy: 8 (over y, x, core).
Axes of the slice: x: 2, y: 2, z: 4, core: 2. Of those that a mesh axis runs over, the one named last changes fastest.
Arguments:
- observed: float32 [2, 8192, 8192], P(None, 'gx', 'gy'), may hold values from -6 to 6
- noise_var: float32 [8192, 8192], P('gx', 'gy'), may hold values from 0.05 to 0.5
- row_kernel: float32 [4096, 4096], P('gx'), may hold values from -1 to 1.2, as said below
- col_kernel: float32 [4096, 4096], P('gy'), may hold values from -1 to 1.2, as said below
Outputs:
- gram_times: float32 [2, 8192, 8192], P(None, 'gx', 'gy')
The draws below stay inside these ranges and needn't reach their ends.
Inputs may be any that keep to these rules, and one draw needn't show every extreme that they name: row_kernel is symmetric. col_kernel is symmetric.
All inputs are finite; a program needn't handle non-finite values.
Results may differ from the reference program's by a relative error of at most 0.000065.
Values sent between devices are 32-bit elements; how exact they have to be, the bound alone decides.
A program may use at most 192 MiB of HBM per device.

```python
import math
import jax
import jax.numpy as jnp
from jax import lax

MX = 4096
MY = 4096
RHS = 2
NXO = 8192
NYO = 8192


def symmetric_kernel(key, order):
    base = jax.random.truncated_normal(key, -4.0, 4.0, (order, order), jnp.float32)
    offdiag = (base + base.T) * (0.3 / math.sqrt(2.0 * order))
    diagonal = jax.random.uniform(jax.random.fold_in(key, 7), (order,), jnp.float32, 0.8, 1.2)
    identity = jnp.eye(order, dtype=jnp.float32)
    return offdiag * (1.0 - identity) + identity * diagonal[None, :]


def draw_row_kernel(key, part):
    return symmetric_kernel(jax.random.fold_in(key, 11), MX)


def draw_col_kernel(key, part):
    return symmetric_kernel(jax.random.fold_in(key, 23), MY)


def shard_levels(key, shape, pieces, least, largest):
    def one(position, blocks):
        steps = jax.random.uniform(jax.random.fold_in(jax.random.fold_in(key, 6), position), (blocks,), jnp.float32, least / len(pieces), largest / len(pieces))
        return jnp.repeat(jnp.exp(steps), shape[position] // blocks).reshape((-1,) + (1,) * (len(shape) - position - 1))

    gain = one(*pieces[0])
    for cut in pieces[1:]:
        gain = gain * one(*cut)
    return gain


def gaussian(key, shape, scale, most, cuts=(), kind=jnp.bfloat16):
    gain = shard_levels(key, shape, cuts, -0.22, 0.18) if cuts else 1.0
    entries = jax.random.normal(key, shape, jnp.float32) * scale * gain
    return jnp.minimum(jnp.maximum(entries, -most), most).astype(kind)


def setup_inputs(seed: int = 0) -> dict:
    keys = jax.random.split(jax.random.key(seed), 5)
    return {
        "observed": gaussian(keys[0], (RHS, NXO, NYO), 1.0, 6.0, ((1, 4), (2, 8)), jnp.float32),
        "noise_var": jnp.clip(jnp.exp(math.log(0.5) - 2.3025851 * jax.random.uniform(keys[1], (NXO, NYO), jnp.float32) ** shard_levels(keys[1], (NXO, NYO), ((0, 4), (1, 8)), -0.2, 0.2)), 0.05, 0.5),
        "row_kernel": draw_row_kernel(jax.random.fold_in(keys[4], 71), 0),
        "col_kernel": draw_col_kernel(jax.random.fold_in(keys[4], 71), 0),
    }


even_taps = (-0.0703125, 0.8671875, 0.2265625, -0.0234375)
odd_taps = (-0.0234375, 0.2265625, 0.8671875, -0.0703125)


def adjoint_rows(extended, count):
    evens = extended[:, 0::2]
    odds = extended[:, 1::2]
    total = jnp.zeros((extended.shape[0], count, extended.shape[2]), jnp.float32)
    for index in range(4):
        start = 3 - index
        total = total + even_taps[index] * evens[:, start:start + count] + odd_taps[index] * odds[:, start:start + count]
    return total


def forward_rows(extended, count):
    first = jnp.zeros((extended.shape[0], count, extended.shape[2]), jnp.float32)
    second = jnp.zeros((extended.shape[0], count, extended.shape[2]), jnp.float32)
    for index in range(4):
        start = index + 1
        first = first + even_taps[index] * extended[:, start:start + count]
        second = second + odd_taps[index] * extended[:, start:start + count]
    stacked = jnp.stack([first, second], axis=2)
    return stacked.reshape(extended.shape[0], 2 * count, extended.shape[2])


def swap_last(field):
    return jnp.transpose(field, (0, 2, 1))


def reference(observed, noise_var, row_kernel, col_kernel):
    padded = jnp.pad(observed, ((0, 0), (4, 4), (0, 0)))
    rowsum = adjoint_rows(padded, MX)
    padded = jnp.pad(swap_last(rowsum), ((0, 0), (4, 4), (0, 0)))
    inducing = swap_last(adjoint_rows(padded, MY))
    mixed = jnp.einsum("rik,jk->rij", inducing, col_kernel, precision=lax.Precision.HIGHEST)
    product = jnp.einsum("ik,rkj->rij", row_kernel, mixed, precision=lax.Precision.HIGHEST)
    padded = jnp.pad(swap_last(product), ((0, 0), (2, 2), (0, 0)))
    colpass = swap_last(forward_rows(padded, MY))
    padded = jnp.pad(colpass, ((0, 0), (2, 2), (0, 0)))
    result = forward_rows(padded, MX)
    return result + noise_var[None] * observed
```

```python
import jax
import jax.numpy as jnp
from jax import lax
from jax.experimental import pallas as pl
from jax.experimental.pallas import tpu as pltpu
from jax.sharding import PartitionSpec as P

PAD = 8
BAND = 256
VMEM_BYTES = 48 * 1024 * 1024


def keys_weight(dist):
    span = jnp.abs(dist)
    inner = (1.5 * span - 2.5) * span * span + 1.0
    outer = ((-0.5 * span + 2.5) * span - 4.0) * span + 2.0
    return jnp.where(span < 1.0, inner, jnp.where(span < 2.0, outer, 0.0))


def weights(coarse, fine):
    return keys_weight(coarse - (fine * 0.5 + 0.25)).astype(jnp.bfloat16)


def positions(size, offset):
    return jnp.arange(size, dtype=jnp.float32) + offset


def halo_positions(width, cols):
    lane = jnp.arange(128)
    place = jnp.where(lane < width, lane - width, cols + lane - width)
    far = jnp.where(lane < 2 * width, place, -1000000)
    return far.astype(jnp.float32)


def neighbours(cells, axis, dim, width):
    count = lax.axis_size(axis)
    head = lax.slice_in_dim(cells, 0, width, axis=dim)
    tail = lax.slice_in_dim(cells, cells.shape[dim] - width, cells.shape[dim], axis=dim)
    before = lax.ppermute(tail, axis, [(i, i + 1) for i in range(count - 1)])
    after = lax.ppermute(head, axis, [(i + 1, i) for i in range(count - 1)])
    return before, after


def side_strips(cells, above, below, width):
    strip_first = jnp.concatenate([part[..., :width] for part in (above, cells, below)], axis=1)
    strip_last = jnp.concatenate([part[..., -width:] for part in (above, cells, below)], axis=1)
    count = lax.axis_size("gy")
    left = lax.ppermute(strip_last, "gy", [(i, i + 1) for i in range(count - 1)])
    right = lax.ppermute(strip_first, "gy", [(i + 1, i) for i in range(count - 1)])
    both = jnp.concatenate([left, right], axis=2)
    return jnp.pad(both, ((0, 0), (0, 0), (0, 128 - 2 * width)))


def split(value):
    high = value.astype(jnp.bfloat16)
    return high, (value - high.astype(jnp.float32)).astype(jnp.bfloat16)


def exact_left(table, value):
    high, low = split(value)
    return jnp.dot(table, high, preferred_element_type=jnp.float32) + jnp.dot(
        table, low, preferred_element_type=jnp.float32
    )


def exact_right(value, table):
    high, low = split(value)
    return jnp.dot(high, table, preferred_element_type=jnp.float32) + jnp.dot(
        low, table, preferred_element_type=jnp.float32
    )


def extended_rows(main, before, after, above, below):
    step = pl.program_id(1)
    first = jnp.where(step == 0, above[0], before[0])
    last = jnp.where(step == pl.num_programs(1) - 1, below[0], after[0])
    return jnp.concatenate([first, main[0], last], axis=0)


def adjoint_kernel(main, before, after, above, below, sides, row_table, col_table, side_table, out):
    step = pl.program_id(1)
    cells = extended_rows(main, before, after, above, below)
    rows = exact_left(row_table[...], cells)
    start = pl.multiple_of(step * 2 * BAND, 2 * BAND)
    edge = exact_left(row_table[...], sides[0, pl.ds(start, 2 * BAND + 2 * PAD), :])
    out[0] = exact_right(rows, col_table[...]) + exact_right(edge, side_table[...])


def forward_kernel(
    main, before, after, above, below, sides, row_table, col_table, side_table, noise, observed, out
):
    step = pl.program_id(1)
    cells = extended_rows(main, before, after, above, below)
    start = pl.multiple_of(step * BAND, BAND)
    edge = sides[0, pl.ds(start, BAND + 2 * PAD), :]
    cols = exact_right(cells, col_table[...]) + exact_right(edge, side_table[...])
    out[0] = exact_left(row_table[...], cols) + noise[...] * observed[0]


def banded_specs(rows, cols, band):
    per = band // PAD
    last = rows // PAD - 1
    return [
        pl.BlockSpec((1, band, cols), lambda r, i: (r, i, 0)),
        pl.BlockSpec((1, PAD, cols), lambda r, i: (r, jnp.maximum(i * per - 1, 0), 0)),
        pl.BlockSpec((1, PAD, cols), lambda r, i: (r, jnp.minimum((i + 1) * per, last), 0)),
        pl.BlockSpec((1, PAD, cols), lambda r, i: (r, 0, 0)),
        pl.BlockSpec((1, PAD, cols), lambda r, i: (r, 0, 0)),
        pl.BlockSpec((1, rows + 2 * PAD, 128), lambda r, i: (r, 0, 0)),
    ]


def whole(table):
    return pl.BlockSpec(table.shape, lambda r, i: (0, 0))


def adjoint(observed):
    rhs, rows, cols = observed.shape
    above, below = neighbours(observed, "gx", 1, PAD)
    sides = side_strips(observed, above, below, 4)
    coarse = cols // 2
    row_table = weights(positions(BAND, 0)[:, None], positions(2 * BAND + 2 * PAD, -PAD)[None, :])
    col_table = weights(positions(coarse, 0)[None, :], positions(cols, 0)[:, None])
    side_table = weights(positions(coarse, 0)[None, :], halo_positions(4, cols)[:, None])
    return pl.pallas_call(
        adjoint_kernel,
        grid=(rhs, rows // (2 * BAND)),
        in_specs=banded_specs(rows, cols, 2 * BAND)
        + [whole(row_table), whole(col_table), whole(side_table)],
        out_specs=pl.BlockSpec((1, BAND, coarse), lambda r, i: (r, i, 0)),
        out_shape=jax.ShapeDtypeStruct((rhs, rows // 2, coarse), jnp.float32),
        compiler_params=pltpu.CompilerParams(vmem_limit_bytes=VMEM_BYTES),
    )(observed, observed, observed, above, below, sides, row_table, col_table, side_table)


def forward(product, noise_var, observed):
    rhs, rows, cols = product.shape
    above, below = neighbours(product, "gx", 1, PAD)
    sides = side_strips(product, above, below, 2)
    fine = 2 * cols
    row_table = weights(positions(BAND + 2 * PAD, -PAD)[None, :], positions(2 * BAND, 0)[:, None])
    col_table = weights(positions(cols, 0)[:, None], positions(fine, 0)[None, :])
    side_table = weights(halo_positions(2, cols)[:, None], positions(fine, 0)[None, :])
    return pl.pallas_call(
        forward_kernel,
        grid=(rhs, rows // BAND),
        in_specs=banded_specs(rows, cols, BAND)
        + [
            whole(row_table),
            whole(col_table),
            whole(side_table),
            pl.BlockSpec((2 * BAND, fine), lambda r, i: (i, 0)),
            pl.BlockSpec((1, 2 * BAND, fine), lambda r, i: (r, i, 0)),
        ],
        out_specs=pl.BlockSpec((1, 2 * BAND, fine), lambda r, i: (r, i, 0)),
        out_shape=jax.ShapeDtypeStruct((rhs, 2 * rows, fine), jnp.float32),
        compiler_params=pltpu.CompilerParams(vmem_limit_bytes=VMEM_BYTES),
    )(
        product, product, product, above, below, sides,
        row_table, col_table, side_table, noise_var, observed,
    )


def by_columns(field, col_kernel):
    gathered = lax.all_gather(field, "gy", axis=1, tiled=True)
    return jnp.einsum("ik,jk->ij", gathered, col_kernel, precision=lax.Precision.HIGH)


def by_rows(field, row_kernel):
    gathered = lax.all_gather(field, "gx", axis=0, tiled=True)
    return jnp.einsum("ik,kj->ij", row_kernel, gathered, precision=lax.Precision.HIGH)


def body(observed, noise_var, row_kernel, col_kernel):
    inducing = adjoint(observed)
    one = by_rows(by_columns(inducing[0], col_kernel), row_kernel)
    two = by_columns(by_rows(inducing[1], row_kernel), col_kernel)
    return forward(jnp.stack([one, two]), noise_var, observed)


def solution(mesh):
    return jax.shard_map(
        body,
        mesh=mesh,
        in_specs=(P(None, "gx", "gy"), P("gx", "gy"), P("gx", None), P("gy", None)),
        out_specs=P(None, "gx", "gy"),
        check_vma=False,
    )
```

```python
import jax
import jax.numpy as jnp
from jax import lax
from jax.experimental import pallas as pl
from jax.experimental.pallas import tpu as pltpu
from jax.sharding import PartitionSpec as P

PAD = 8
BAND = 256
VMEM_BYTES = 48 * 1024 * 1024


def keys_weight(dist):
    span = jnp.abs(dist)
    inner = (1.5 * span - 2.5) * span * span + 1.0
    outer = ((-0.5 * span + 2.5) * span - 4.0) * span + 2.0
    return jnp.where(span < 1.0, inner, jnp.where(span < 2.0, outer, 0.0))


def weights(coarse, fine):
    return keys_weight(coarse - (fine * 0.5 + 0.25)).astype(jnp.bfloat16)


def positions(size, offset):
    return jnp.arange(size, dtype=jnp.float32) + offset


def halo_positions(width, cols):
    lane = jnp.arange(128)
    place = jnp.where(lane < width, lane - width, cols + lane - width)
    far = jnp.where(lane < 2 * width, place, -1000000)
    return far.astype(jnp.float32)


def neighbours(cells, axis, dim, width):
    count = lax.axis_size(axis)
    head = lax.slice_in_dim(cells, 0, width, axis=dim)
    tail = lax.slice_in_dim(cells, cells.shape[dim] - width, cells.shape[dim], axis=dim)
    before = lax.ppermute(tail, axis, [(i, i + 1) for i in range(count - 1)])
    after = lax.ppermute(head, axis, [(i + 1, i) for i in range(count - 1)])
    return before, after


def side_strips(cells, above, below, width):
    strip_first = jnp.concatenate([part[..., :width] for part in (above, cells, below)], axis=1)
    strip_last = jnp.concatenate([part[..., -width:] for part in (above, cells, below)], axis=1)
    count = lax.axis_size("gy")
    left = lax.ppermute(strip_last, "gy", [(i, i + 1) for i in range(count - 1)])
    right = lax.ppermute(strip_first, "gy", [(i + 1, i) for i in range(count - 1)])
    both = jnp.concatenate([left, right], axis=2)
    return jnp.pad(both, ((0, 0), (0, 0), (0, 128 - 2 * width)))


def split(value):
    high = value.astype(jnp.bfloat16)
    return high, (value - high.astype(jnp.float32)).astype(jnp.bfloat16)


def exact_left(table, value):
    high, low = split(value)
    return jnp.dot(table, high, preferred_element_type=jnp.float32) + jnp.dot(
        table, low, preferred_element_type=jnp.float32
    )


def exact_right(value, table):
    high, low = split(value)
    return jnp.dot(high, table, preferred_element_type=jnp.float32) + jnp.dot(
        low, table, preferred_element_type=jnp.float32
    )


def extended_rows(main, before, after, above, below):
    step = pl.program_id(1)
    first = jnp.where(step == 0, above[0], before[0])
    last = jnp.where(step == pl.num_programs(1) - 1, below[0], after[0])
    return jnp.concatenate([first, main[0], last], axis=0)


def adjoint_kernel(main, before, after, above, below, sides, row_table, col_table, side_table, out):
    step = pl.program_id(1)
    cells = extended_rows(main, before, after, above, below)
    rows = exact_left(row_table[...], cells)
    start = pl.multiple_of(step * 2 * BAND, 2 * BAND)
    edge = exact_left(row_table[...], sides[0, pl.ds(start, 2 * BAND + 2 * PAD), :])
    out[0] = exact_right(rows, col_table[...]) + exact_right(edge, side_table[...])


def forward_kernel(
    main, before, after, above, below, sides, row_table, col_table, side_table, noise, observed, out
):
    step = pl.program_id(1)
    cells = extended_rows(main, before, after, above, below)
    start = pl.multiple_of(step * BAND, BAND)
    edge = sides[0, pl.ds(start, BAND + 2 * PAD), :]
    cols = exact_right(cells, col_table[...]) + exact_right(edge, side_table[...])
    out[0] = exact_left(row_table[...], cols) + noise[...] * observed[0]


def banded_specs(rows, cols, band, source):
    per = band // PAD
    last = rows // PAD - 1
    return [
        pl.BlockSpec((1, band, cols), lambda r, i: (source, i, 0)),
        pl.BlockSpec((1, PAD, cols), lambda r, i: (source, jnp.maximum(i * per - 1, 0), 0)),
        pl.BlockSpec((1, PAD, cols), lambda r, i: (source, jnp.minimum((i + 1) * per, last), 0)),
        pl.BlockSpec((1, PAD, cols), lambda r, i: (source, 0, 0)),
        pl.BlockSpec((1, PAD, cols), lambda r, i: (source, 0, 0)),
        pl.BlockSpec((1, rows + 2 * PAD, 128), lambda r, i: (source, 0, 0)),
    ]


def whole(table):
    return pl.BlockSpec(table.shape, lambda r, i: (0, 0))


def cost(flops, moved):
    return pl.CostEstimate(flops=flops, bytes_accessed=moved, transcendentals=0)


def adjoint(observed):
    rhs, rows, cols = observed.shape
    above, below = neighbours(observed, "gx", 1, PAD)
    sides = side_strips(observed, above, below, 4)
    coarse = cols // 2
    row_table = weights(positions(BAND, 0)[:, None], positions(2 * BAND + 2 * PAD, -PAD)[None, :])
    col_table = weights(positions(coarse, 0)[None, :], positions(cols, 0)[:, None])
    side_table = weights(positions(coarse, 0)[None, :], halo_positions(4, cols)[:, None])

    def one(source, earlier):
        table = side_table
        if earlier is not None:
            table, _ = lax.optimization_barrier((side_table, earlier))
        return pl.pallas_call(
            adjoint_kernel,
            grid=(1, rows // (2 * BAND)),
            in_specs=banded_specs(rows, cols, 2 * BAND, source)
            + [whole(row_table), whole(col_table), whole(side_table)],
            out_specs=pl.BlockSpec((1, BAND, coarse), lambda r, i: (0, i, 0)),
            out_shape=jax.ShapeDtypeStruct((1, rows // 2, coarse), jnp.float32),
            compiler_params=pltpu.CompilerParams(vmem_limit_bytes=VMEM_BYTES),
            cost_estimate=cost(4 * rows * cols * (BAND + coarse), 5 * rows * cols),
        )(observed, observed, observed, above, below, sides, row_table, col_table, table)[0]

    return one


def forward(product, target, noise_var, observed, partial):
    product = product[None]
    _, rows, cols = product.shape
    above, below = neighbours(product, "gx", 1, PAD)
    sides = side_strips(product, above, below, 2)
    fine = 2 * cols
    row_table = weights(positions(BAND + 2 * PAD, -PAD)[None, :], positions(2 * BAND, 0)[:, None])
    col_table = weights(positions(cols, 0)[:, None], positions(fine, 0)[None, :])
    side_table = weights(halo_positions(2, cols)[:, None], positions(fine, 0)[None, :])
    operands = [
        product, product, product, above, below, sides,
        row_table, col_table, side_table, noise_var, observed,
    ]
    in_specs = banded_specs(rows, cols, BAND, 0) + [
        whole(row_table),
        whole(col_table),
        whole(side_table),
        pl.BlockSpec((2 * BAND, fine), lambda r, i: (i, 0)),
        pl.BlockSpec((1, 2 * BAND, fine), lambda r, i: (target, i, 0)),
    ]
    kernel, aliases = forward_kernel, {}
    if partial is not None:
        aliases = {len(operands): 0}
        operands.append(partial)
        in_specs.append(pl.BlockSpec(memory_space=pl.ANY))

        def kernel(*refs):
            forward_kernel(*refs[:11], refs[12])

    return pl.pallas_call(
        kernel,
        grid=(1, rows // BAND),
        in_specs=in_specs,
        out_specs=pl.BlockSpec((1, 2 * BAND, fine), lambda r, i: (target, i, 0)),
        out_shape=jax.ShapeDtypeStruct(observed.shape, jnp.float32),
        input_output_aliases=aliases,
        compiler_params=pltpu.CompilerParams(vmem_limit_bytes=VMEM_BYTES),
        cost_estimate=cost(4 * rows * fine * (cols + 2 * BAND), 26 * rows * fine),
    )(*operands)


def by_columns(field, col_kernel):
    gathered = lax.all_gather(field, "gy", axis=1, tiled=True)
    return jnp.einsum("ik,jk->ij", gathered, col_kernel, precision=lax.Precision.HIGH)


def exchange(field):
    count = lax.axis_size("gx")
    from_left, from_right = [field], [field]
    for step in range(1, count):
        up = [(i, i + 1) for i in range(step - 1, count - 1)]
        down = [(i + 1, i) for i in range(count - step)]
        from_left.append(lax.ppermute(from_left[-1], "gx", up))
        from_right.append(lax.ppermute(from_right[-1], "gx", down))
    return from_left, from_right


def row_products(from_left, from_right, row_kernel):
    count, place = lax.axis_size("gx"), lax.axis_index("gx")
    depth = from_left[0].shape[0]
    total = None
    for step in range(count):
        block = from_left[0]
        if step:
            block = jnp.where(place + step < count, from_right[step], from_left[count - step])
        owner = lax.rem(place + step, count)
        part = lax.dynamic_slice_in_dim(row_kernel, owner * depth, depth, axis=1)
        term = jnp.einsum("ik,kj->ij", part, block, precision=lax.Precision.HIGH)
        total = term if total is None else total + term
    return total


def body(observed, noise_var, row_kernel, col_kernel):
    inducing = adjoint(observed)
    rows_first = inducing(1, None)
    cols_first = inducing(0, rows_first)
    from_left, from_right = exchange(rows_first)
    mixed_cols = by_columns(cols_first, col_kernel)
    from_left[-1], from_right[-1], mixed_cols = lax.optimization_barrier(
        (from_left[-1], from_right[-1], mixed_cols)
    )
    again = exchange(mixed_cols)
    two = by_columns(row_products(from_left, from_right, row_kernel), col_kernel)
    partial = forward(two, 1, noise_var, observed, None)
    one = row_products(*again, row_kernel)
    return forward(one, 0, noise_var, observed, partial)


def solution(mesh):
    return jax.shard_map(
        body,
        mesh=mesh,
        in_specs=(P(None, "gx", "gy"), P("gx", "gy"), P("gx", None), P("gy", None)),
        out_specs=P(None, "gx", "gy"),
        check_vma=False,
    )
```
